32 devices in a mesh: ctx: 8 (over z, x), tp: 4 (over y, core).
Axes of the slice: x: 2, y: 2, z: 4, core: 2. Of those that a mesh axis runs over, the one named last changes fastest.
Arguments:
- tokens: bfloat16 [4096, 3072], P(('ctx', 'tp')), may hold values from -6 to 6
- w_query: bfloat16 [3072, 4096], P(None, 'tp'), may hold values from -0.109375 to 0.109375
- w_key: bfloat16 [3072, 4096], P(None, 'tp'), may hold values from -0.109375 to 0.109375
- w_value: bfloat16 [3072, 4096], P(None, 'tp'), may hold values from -0.109375 to 0.109375
- norm_gain: float32 [4096], P('tp'), may hold values from 0.1 to 1.9
Outputs:
- attended: bfloat16 [4096, 4096], P('ctx', 'tp')
The draws below stay inside these ranges and needn't reach their ends.
All inputs are finite; a program needn't handle non-finite values.
Results may differ from the reference program's by a relative error of at most 0.0062.
Values may be sent and summed in bfloat16 or wider, within the bound.
A program may use at most 64 MiB of HBM per device.

```python
import jax
import jax.numpy as jnp
from jax import lax

D = 3072
HEADS = 32
HEAD_DIM = 128
BLOCK = 512
TOKENS = 4096


def levels(own_key, shape, split, least, largest):
    level = 1.0
    for axis_at, blocks in split:
        heights = jax.random.uniform(jax.random.fold_in(jax.random.fold_in(own_key, 6), axis_at), (blocks,), jnp.float32, least / len(split), largest / len(split))
        level = level * jnp.repeat(jnp.exp(heights), shape[axis_at] // blocks).reshape((-1,) + (1,) * (len(shape) - 1 - axis_at))
    return level


def bell_draw(own_key, extent, width, bound, pieces=(), held_as=jnp.bfloat16):
    loudness = levels(own_key, extent, pieces, -0.22, 0.18) if pieces else 1.0
    values = jax.random.normal(own_key, extent, jnp.float32) * width * loudness
    return jnp.minimum(jnp.maximum(values, -bound), bound).astype(held_as)


def setup_inputs(seed: int = 0) -> dict:
    splits = jax.random.split(jax.random.key(seed), 6)
    return {
        "tokens": bell_draw(splits[0], (TOKENS, D), 1.0, 6.0, ((0, 32),)),
        "w_query": bell_draw(splits[1], (D, HEADS * HEAD_DIM), D ** -0.5, 0.109375, ((1, 4),)),
        "w_key": bell_draw(splits[2], (D, HEADS * HEAD_DIM), D ** -0.5, 0.109375, ((1, 4),)),
        "w_value": bell_draw(splits[3], (D, HEADS * HEAD_DIM), D ** -0.5, 0.109375, ((1, 4),)),
        "norm_gain": jnp.clip(1.0 + 0.18 * jax.random.normal(splits[4], (HEADS * HEAD_DIM,), jnp.float32), 0.1, 1.9),
    }


EPSILON = 1e-06

def reference(tokens, w_query, w_key, w_value, norm_gain):
    query = jnp.dot(tokens, w_query, preferred_element_type=jnp.float32).astype(jnp.bfloat16)
    key_all = jnp.dot(tokens, w_key, preferred_element_type=jnp.float32).astype(jnp.bfloat16)
    value_all = jnp.dot(tokens, w_value, preferred_element_type=jnp.float32).astype(jnp.bfloat16)
    block_count = TOKENS // BLOCK
    query_blocks = query.reshape(block_count, BLOCK, HEADS, HEAD_DIM)
    key_blocks = key_all.reshape(block_count, BLOCK, HEADS, HEAD_DIM)
    value_blocks = value_all.reshape(block_count, BLOCK, HEADS, HEAD_DIM)
    causal = jnp.arange(BLOCK)[:, None] >= jnp.arange(BLOCK)[None, :]
    highest = lax.Precision.HIGHEST

    def advance(state, blocks):
        query_part, key_part, value_part = blocks
        query_wide = query_part.astype(jnp.float32)
        key_wide = key_part.astype(jnp.float32)
        value_wide = value_part.astype(jnp.float32)
        scores = jnp.einsum('qhd,khd->hqk', query_wide, key_wide, precision=highest)
        scores = jnp.where(causal[None], scores, jnp.float32(0.0))
        scores = lax.optimization_barrier(scores.astype(jnp.bfloat16)).astype(jnp.float32)
        inner = jnp.einsum('hqk,khe->qhe', scores, value_wide, precision=highest)
        carried_part = jnp.einsum('qhd,hde->qhe', query_wide, state, precision=highest)
        new_state = state + jnp.einsum('khd,khe->hde', key_wide, value_wide, precision=highest)
        return (new_state, inner + carried_part)
    start_state = jnp.zeros((HEADS, HEAD_DIM, HEAD_DIM), jnp.float32)
    unused, mixed = lax.scan(advance, start_state, (query_blocks, key_blocks, value_blocks))
    mean_square = lax.optimization_barrier(jnp.mean(mixed * mixed, axis=-1, keepdims=True))
    normed = mixed * lax.rsqrt(mean_square + EPSILON) * norm_gain.reshape(HEADS, HEAD_DIM)
    return normed.reshape(TOKENS, HEADS * HEAD_DIM).astype(jnp.bfloat16)
```

```python
import functools

import jax
import jax.numpy as jnp
from jax import lax
from jax.experimental import pallas as pl
from jax.experimental.pallas import tpu as pltpu
from jax.sharding import PartitionSpec as P

HEAD_DIM = 128
BLOCK = 512
EPSILON = 1e-06
MESH = pl.DeviceIdType.MESH
TILE_N = 256
CHUNKS = 6
F32 = jnp.float32
BF16 = jnp.bfloat16


def kernel(
    nctx, ntp, tok, wq, wk, wv, gain, out,
    xbuf, wbuf, acc, kvq, mixed, st, s1, r1, pin, pout, pown, s2, r2,
    wsem, osem, ysend, yrecv, ssend, srecv, fsend, frecv,
    s1send, s1recv, csend, crecv, s2send, s2recv,
):
    ctx, tp = lax.axis_index("ctx"), lax.axis_index("tp")
    rows, depth = tok.shape
    width = wq.shape[1]
    tiles = width // TILE_N
    heads = width // HEAD_DIM
    half = heads // 2
    chips, pairs = ntp // 2, nctx // 2
    core, chip = tp % 2, tp // 2
    sib = tp + 1 - 2 * core
    odd, pair = ctx % 2, ctx // 2
    partner = ctx + 1 - 2 * odd
    ck = depth // CHUNKS
    duo = 2 * rows

    def at_rows(index, count):
        return pl.ds(pl.multiple_of(index * count, count), count)

    weights = (wk, wv, wq)

    def weight_copy(m, n):
        cols = pl.ds(pl.multiple_of(n * TILE_N, TILE_N), TILE_N)
        return pltpu.make_async_copy(
            weights[m].at[:, cols], wbuf.at[m, :, cols], wsem.at[m * tiles + n]
        )

    own = pltpu.make_async_copy(tok, xbuf.at[at_rows(tp, rows), :], osem)
    own.start()
    for m in range(3):
        for n in range(tiles):
            weight_copy(m, n).start()

    barrier = pltpu.get_barrier_semaphore()

    def greet(c, t):
        pl.semaphore_signal(barrier, inc=1, device_id={"ctx": c, "tp": t}, device_id_type=MESH)

    greet(ctx, sib)
    for j in range(1, chips):
        greet(ctx, ((chip + j) % chips) * 2 + core)
    greet(partner, tp)

    @pl.when(pair > 0)
    def _():
        greet(ctx - 2, tp)

    @pl.when(pair < pairs - 1)
    def _():
        greet(ctx + 2, tp)

    inner = jnp.minimum(pair, 1) + jnp.minimum(pairs - 1 - pair, 1)
    pl.semaphore_wait(barrier, chips + 1 + inner)

    def cols_of(c):
        return pl.ds(c * ck, ck)

    def y_copy(j, c, source):
        return pltpu.make_async_remote_copy(
            src_ref=tok.at[:, cols_of(c)],
            dst_ref=xbuf.at[at_rows(source, rows), cols_of(c)],
            send_sem=ysend.at[j - 1, c],
            recv_sem=yrecv.at[j - 1, c],
            device_id={"ctx": ctx, "tp": ((chip + j) % chips) * 2 + core},
            device_id_type=MESH,
        )

    def sib_copy(source):
        return pltpu.make_async_remote_copy(
            src_ref=tok,
            dst_ref=xbuf.at[at_rows(source, rows), :],
            send_sem=ssend,
            recv_sem=srecv,
            device_id={"ctx": ctx, "tp": sib},
            device_id_type=MESH,
        )

    def pass_on(j, c, source):
        place = xbuf.at[at_rows(source, rows), cols_of(c)]
        return pltpu.make_async_remote_copy(
            src_ref=place,
            dst_ref=place,
            send_sem=fsend.at[j - 1, c],
            recv_sem=frecv.at[j - 1, c],
            device_id={"ctx": ctx, "tp": sib},
            device_id_type=MESH,
        )

    sib_copy(tp).start()
    for c in range(CHUNKS):
        for j in range(1, chips):
            y_copy(j, c, tp).start()

    own.wait()
    sib_copy(sib).wait_recv()
    mine = at_rows(chip, duo)
    for m in range(3):

        @pl.loop(0, tiles)
        def _(n, m=m):
            weight_copy(m, n).wait()
            cols = pl.ds(pl.multiple_of(n * TILE_N, TILE_N), TILE_N)
            done = jnp.dot(xbuf[mine, :], wbuf[m, :, cols], preferred_element_type=F32)
            kvq[m, mine, cols] = done.astype(BF16)

    def origin(j):
        return (chip - j + chips) % chips

    def wave(c, low, high):
        for j in range(1, chips):
            there = at_rows(origin(j), duo)

            @pl.loop(low * tiles, high * tiles)
            def _(index):
                m, n = index // tiles, index % tiles
                cols = pl.ds(pl.multiple_of(n * TILE_N, TILE_N), TILE_N)
                term = jnp.dot(
                    xbuf[there, cols_of(c)],
                    wbuf[m, cols_of(c), cols],
                    preferred_element_type=F32,
                )
                if c > 0:
                    term += acc[m, there, cols]
                if c < CHUNKS - 1:
                    acc[m, there, cols] = term
                else:
                    kvq[m, there, cols] = term.astype(BF16)

    for c in range(CHUNKS):
        for j in range(1, chips):
            source = origin(j) * 2 + core
            y_copy(j, c, source).wait_recv()
            pass_on(j, c, source).start()
        for j in range(1, chips):
            pass_on(j, c, origin(j) * 2 + 1 - core).wait_recv()
        if c < CHUNKS - 1:
            wave(c, 0, 3)
        else:
            wave(c, 0, 2)

    def head_cols(h):
        return pl.ds(pl.multiple_of(h * HEAD_DIM, HEAD_DIM), HEAD_DIM)

    def outer(h):
        return lax.dot_general(
            kvq[0, :, head_cols(h)], kvq[1, :, head_cols(h)],
            (((0,), (0,)), ((), ())), preferred_element_type=F32,
        )

    def to_partner(buffer, landing, send, recv, i):
        return pltpu.make_async_remote_copy(
            src_ref=buffer.at[i],
            dst_ref=landing.at[i],
            send_sem=send.at[i],
            recv_sem=recv.at[i],
            device_id={"ctx": partner, "tp": tp},
            device_id_type=MESH,
        )

    def first(i):
        return to_partner(s1, r1, s1send, s1recv, i)

    def second(i):
        return to_partner(s2, r2, s2send, s2recv, i)

    def onward(i):
        return pltpu.make_async_remote_copy(
            src_ref=pout.at[i],
            dst_ref=pin.at[i],
            send_sem=csend.at[i],
            recv_sem=crecv.at[i],
            device_id={"ctx": jnp.minimum(ctx + 2, nctx - 2 + odd), "tp": tp},
            device_id_type=MESH,
        )

    @pl.loop(0, half)
    def _(i):
        s1[i] = outer((1 - odd) * half + i).astype(BF16)
        first(i).start()

    @pl.loop(0, half)
    def _(i):
        st[i] = outer(odd * half + i)

    wave(CHUNKS - 1, 2, 3)

    mid = BLOCK // 2

    def intra(h):
        cols = head_cols(h)
        causal = lax.broadcasted_iota(jnp.int32, (mid, mid), 0) >= lax.broadcasted_iota(
            jnp.int32, (mid, mid), 1
        )
        top, low = pl.ds(0, mid), pl.ds(mid, mid)

        def score(a, b):
            return lax.dot_general(
                kvq[2, a, cols], kvq[0, b, cols],
                (((1,), (1,)), ((), ())), preferred_element_type=F32,
            )

        s00 = jnp.where(causal, score(top, top), 0.0).astype(BF16)
        s10 = score(low, top).astype(BF16)
        s11 = jnp.where(causal, score(low, low), 0.0).astype(BF16)
        v0, v1 = kvq[1, top, cols], kvq[1, low, cols]
        mixed[h, top, :] = jnp.dot(s00, v0, preferred_element_type=F32)
        mixed[h, low, :] = jnp.dot(s10, v0, preferred_element_type=F32) + jnp.dot(
            s11, v1, preferred_element_type=F32
        )

    def finish(h, state):
        cols = head_cols(h)
        full = mixed[h] + jnp.dot(kvq[2, :, cols], state, preferred_element_type=F32)
        mean_square = jnp.mean(full * full, axis=-1, keepdims=True)
        out[:, cols] = (full * lax.rsqrt(mean_square + EPSILON) * gain[pl.ds(h, 1), :]).astype(BF16)

    @pl.when(pair == 0)
    def _():
        pin[...] = jnp.zeros_like(pin)

    ahead = jnp.minimum(2 * pair, heads)

    @pl.loop(0, ahead)
    def _(h):
        intra(h)

    @pl.loop(0, half)
    def _(i):
        first(i).wait_recv()

        @pl.when(pair > 0)
        def _():
            onward(i).wait_recv()

        before = pin[i].astype(F32)
        here, beside = st[i], r1[i].astype(F32)

        @pl.when(pair < pairs - 1)
        def _():
            pout[i] = (before + here + beside).astype(BF16)
            onward(i).start()

        s2[i] = (before + jnp.where(odd == 0, here, 0.0)).astype(BF16)
        second(i).start()
        pown[i] = (before + jnp.where(odd == 1, beside, 0.0)).astype(BF16)

        @pl.loop(jnp.minimum(ahead + 2 * i, heads), jnp.minimum(ahead + 2 * i + 2, heads))
        def _(h):
            intra(h)

    @pl.loop(0, half)
    def _(i):
        finish(odd * half + i, pown[i])

    @pl.loop(0, half)
    def _(i):
        second(i).wait_recv()
        finish((1 - odd) * half + i, r2[i])

    sib_copy(tp).wait_send()
    for c in range(CHUNKS):
        for j in range(1, chips):
            y_copy(j, c, tp).wait_send()
            pass_on(j, c, origin(j) * 2 + core).wait_send()

    @pl.loop(0, half)
    def _(i):
        first(i).wait_send()
        second(i).wait_send()

        @pl.when(pair < pairs - 1)
        def _():
            onward(i).wait_send()


def body(nctx, ntp, tokens, w_query, w_key, w_value, norm_gain):
    rows, depth = tokens.shape
    width = w_query.shape[1]
    heads = width // HEAD_DIM
    half, chips = heads // 2, ntp // 2
    tiles = width // TILE_N
    assert rows * ntp == BLOCK
    anywhere = pl.BlockSpec(memory_space=pl.ANY)
    vmem = pl.BlockSpec(memory_space=pltpu.VMEM)
    dma = pltpu.SemaphoreType.DMA
    small = pltpu.VMEM((half, HEAD_DIM, HEAD_DIM), BF16)
    hops = (max(chips - 1, 1), CHUNKS)
    return pl.pallas_call(
        functools.partial(kernel, nctx, ntp),
        out_shape=jax.ShapeDtypeStruct((BLOCK, width), BF16),
        in_specs=[anywhere] * 4 + [vmem],
        out_specs=vmem,
        scratch_shapes=[
            pltpu.VMEM((BLOCK, depth), BF16),
            pltpu.VMEM((3, depth, width), BF16),
            pltpu.VMEM((3, BLOCK, width), F32),
            pltpu.VMEM((3, BLOCK, width), BF16),
            pltpu.VMEM((heads, BLOCK, HEAD_DIM), F32),
            pltpu.VMEM((half, HEAD_DIM, HEAD_DIM), F32),
            small, small, small, small, small, small, small,
            dma((3 * tiles,)), dma, dma(hops), dma(hops), dma, dma, dma(hops), dma(hops),
            dma((half,)), dma((half,)), dma((half,)), dma((half,)), dma((half,)), dma((half,)),
        ],
        compiler_params=pltpu.CompilerParams(
            collective_id=0, has_side_effects=True, vmem_limit_bytes=60 * 2**20
        ),
        cost_estimate=pl.CostEstimate(
            flops=2 * BLOCK * depth * 3 * width, bytes_accessed=6 * depth * width, transcendentals=0
        ),
    )(tokens, w_query, w_key, w_value, norm_gain.reshape(heads, HEAD_DIM))


def solution(mesh):
    placed = (P(("ctx", "tp"), None), P(None, "tp"), P(None, "tp"), P(None, "tp"), P("tp"))
    return jax.shard_map(
        functools.partial(body, mesh.shape["ctx"], mesh.shape["tp"]),
        mesh=mesh, in_specs=placed, out_specs=P("ctx", "tp"), check_vma=False,
    )
```

```python
import functools

import jax
import jax.numpy as jnp
from jax import lax
from jax.experimental import pallas as pl
from jax.experimental.pallas import tpu as pltpu
from jax.sharding import PartitionSpec as P

HEAD_DIM = 128
BLOCK = 512
EPSILON = 1e-06
MESH = pl.DeviceIdType.MESH
TILE_N = 512
TWELFTHS = (0, 4, 8, 10, 11, 12)
CHUNKS = len(TWELFTHS) - 1
F32 = jnp.float32
BF16 = jnp.bfloat16


def kernel(
    nctx, ntp, tok, wq, wk, wv, gain, out,
    xbuf, wbuf, acc, kvq, mixed, st, s1, r1, pin, pout, pown, s2, r2,
    wsem, osem, ysend, yrecv, ssend, srecv, fsend, frecv,
    s1send, s1recv, csend, crecv, s2send, s2recv,
):
    ctx, tp = lax.axis_index("ctx"), lax.axis_index("tp")
    rows, depth = tok.shape
    width = wq.shape[1]
    tiles = width // TILE_N
    heads = width // HEAD_DIM
    half = heads // 2
    chips, pairs = ntp // 2, nctx // 2
    core, chip = tp % 2, tp // 2
    sib = tp + 1 - 2 * core
    odd, pair = ctx % 2, ctx // 2
    partner = ctx + 1 - 2 * odd
    cuts = [depth * part // 12 for part in TWELFTHS]
    duo = 2 * rows

    def at_rows(index, count):
        return pl.ds(pl.multiple_of(index * count, count), count)

    weights = (wk, wv, wq)

    def weight_copy(m, n):
        cols = pl.ds(pl.multiple_of(n * TILE_N, TILE_N), TILE_N)
        return pltpu.make_async_copy(
            weights[m].at[:, cols], wbuf.at[m, :, cols], wsem.at[m * tiles + n]
        )

    own = pltpu.make_async_copy(tok, xbuf.at[at_rows(tp, rows), :], osem)
    own.start()
    for m in range(3):
        for n in range(tiles):
            weight_copy(m, n).start()

    barrier = pltpu.get_barrier_semaphore()

    def greet(c, t):
        pl.semaphore_signal(barrier, inc=1, device_id={"ctx": c, "tp": t}, device_id_type=MESH)

    greet(ctx, sib)
    for j in range(1, chips):
        greet(ctx, ((chip + j) % chips) * 2 + core)
    greet(partner, tp)

    @pl.when(pair > 0)
    def _():
        greet(ctx - 2, tp)

    @pl.when(pair < pairs - 1)
    def _():
        greet(ctx + 2, tp)

    inner = jnp.minimum(pair, 1) + jnp.minimum(pairs - 1 - pair, 1)
    pl.semaphore_wait(barrier, chips + 1 + inner)

    def cols_of(c):
        return pl.ds(cuts[c], cuts[c + 1] - cuts[c])

    def y_copy(j, c, source):
        return pltpu.make_async_remote_copy(
            src_ref=tok.at[:, cols_of(c)],
            dst_ref=xbuf.at[at_rows(source, rows), cols_of(c)],
            send_sem=ysend.at[j - 1, c],
            recv_sem=yrecv.at[j - 1, c],
            device_id={"ctx": ctx, "tp": ((chip + j) % chips) * 2 + core},
            device_id_type=MESH,
        )

    def sib_copy(source):
        return pltpu.make_async_remote_copy(
            src_ref=tok,
            dst_ref=xbuf.at[at_rows(source, rows), :],
            send_sem=ssend,
            recv_sem=srecv,
            device_id={"ctx": ctx, "tp": sib},
            device_id_type=MESH,
        )

    def pass_on(j, c, source):
        place = xbuf.at[at_rows(source, rows), cols_of(c)]
        return pltpu.make_async_remote_copy(
            src_ref=place,
            dst_ref=place,
            send_sem=fsend.at[j - 1, c],
            recv_sem=frecv.at[j - 1, c],
            device_id={"ctx": ctx, "tp": sib},
            device_id_type=MESH,
        )

    sib_copy(tp).start()
    for c in range(CHUNKS):
        for j in range(1, chips):
            y_copy(j, c, tp).start()

    own.wait()
    sib_copy(sib).wait_recv()
    mine = at_rows(chip, duo)
    for m in range(3):

        @pl.loop(0, tiles)
        def _(n, m=m):
            weight_copy(m, n).wait()
            cols = pl.ds(pl.multiple_of(n * TILE_N, TILE_N), TILE_N)
            done = jnp.dot(xbuf[mine, :], wbuf[m, :, cols], preferred_element_type=F32)
            kvq[m, mine, cols] = done.astype(BF16)

    def head_cols(h):
        return pl.ds(pl.multiple_of(h * HEAD_DIM, HEAD_DIM), HEAD_DIM)

    def outer(h, where):
        return lax.dot_general(
            kvq[0, where, head_cols(h)], kvq[1, where, head_cols(h)],
            (((0,), (0,)), ((), ())), preferred_element_type=F32,
        )

    def whole_outer(h):
        total = st[h]
        for j in range(1, chips):
            total += outer(h, at_rows(origin(j), duo))
        return total

    @pl.loop(0, heads)
    def _(h):
        st[h] = outer(h, mine)

    def origin(j):
        return (chip - j + chips) % chips

    def wave(c, low, high):
        for j in range(1, chips):
            there = at_rows(origin(j), duo)

            @pl.loop(low, high)
            def _(m):
                term = jnp.dot(
                    xbuf[there, cols_of(c)], wbuf[m, cols_of(c), :], preferred_element_type=F32
                )
                if c > 0:
                    term += acc[m, there, :]
                if c < CHUNKS - 1:
                    acc[m, there, :] = term
                else:
                    kvq[m, there, :] = term.astype(BF16)

    for c in range(CHUNKS):
        for j in range(1, chips):
            source = origin(j) * 2 + core
            y_copy(j, c, source).wait_recv()
            pass_on(j, c, source).start()
        for j in range(1, chips):
            pass_on(j, c, origin(j) * 2 + 1 - core).wait_recv()
        if c < CHUNKS - 1:
            wave(c, 0, 3)
        else:
            wave(c, 0, 2)

    def to_partner(buffer, landing, send, recv, i):
        return pltpu.make_async_remote_copy(
            src_ref=buffer.at[i],
            dst_ref=landing.at[i],
            send_sem=send.at[i],
            recv_sem=recv.at[i],
            device_id={"ctx": partner, "tp": tp},
            device_id_type=MESH,
        )

    def first(i):
        return to_partner(s1, r1, s1send, s1recv, i)

    def second(i):
        return to_partner(s2, r2, s2send, s2recv, i)

    def onward(i):
        return pltpu.make_async_remote_copy(
            src_ref=pout.at[i],
            dst_ref=pin.at[i],
            send_sem=csend.at[i],
            recv_sem=crecv.at[i],
            device_id={"ctx": jnp.minimum(ctx + 2, nctx - 2 + odd), "tp": tp},
            device_id_type=MESH,
        )

    @pl.loop(0, half)
    def _(i):
        s1[i] = whole_outer((1 - odd) * half + i).astype(BF16)
        first(i).start()

    @pl.loop(0, half)
    def _(i):
        h = odd * half + i
        st[h] = whole_outer(h)

    wave(CHUNKS - 1, 2, 3)

    mid = BLOCK // 2

    def intra(h):
        cols = head_cols(h)
        causal = lax.broadcasted_iota(jnp.int32, (mid, mid), 0) >= lax.broadcasted_iota(
            jnp.int32, (mid, mid), 1
        )
        top, low = pl.ds(0, mid), pl.ds(mid, mid)

        def score(a, b):
            return lax.dot_general(
                kvq[2, a, cols], kvq[0, b, cols],
                (((1,), (1,)), ((), ())), preferred_element_type=F32,
            )

        s00 = jnp.where(causal, score(top, top), 0.0).astype(BF16)
        s10 = score(low, top).astype(BF16)
        s11 = jnp.where(causal, score(low, low), 0.0).astype(BF16)
        v0, v1 = kvq[1, top, cols], kvq[1, low, cols]
        mixed[h, top, :] = jnp.dot(s00, v0, preferred_element_type=F32)
        mixed[h, low, :] = jnp.dot(s10, v0, preferred_element_type=F32) + jnp.dot(
            s11, v1, preferred_element_type=F32
        )

    def finish(h, state):
        cols = head_cols(h)
        full = mixed[h] + jnp.dot(kvq[2, :, cols], state, preferred_element_type=F32)
        mean_square = jnp.mean(full * full, axis=-1, keepdims=True)
        out[:, cols] = (full * lax.rsqrt(mean_square + EPSILON) * gain[pl.ds(h, 1), :]).astype(BF16)

    @pl.when(pair == 0)
    def _():
        pin[...] = jnp.zeros_like(pin)

    ahead = jnp.minimum(2 * pair, heads)

    @pl.loop(0, ahead)
    def _(h):
        intra(h)

    @pl.loop(0, half)
    def _(i):
        first(i).wait_recv()

        @pl.when(pair > 0)
        def _():
            onward(i).wait_recv()

        before = pin[i].astype(F32)
        here, beside = st[odd * half + i], r1[i].astype(F32)

        @pl.when(pair < pairs - 1)
        def _():
            pout[i] = (before + here + beside).astype(BF16)
            onward(i).start()

        s2[i] = (before + jnp.where(odd == 0, here, 0.0)).astype(BF16)
        second(i).start()
        pown[i] = (before + jnp.where(odd == 1, beside, 0.0)).astype(BF16)

        @pl.loop(jnp.minimum(ahead + 2 * i, heads), jnp.minimum(ahead + 2 * i + 2, heads))
        def _(h):
            intra(h)

    @pl.loop(0, half)
    def _(i):
        finish(odd * half + i, pown[i])

    @pl.loop(0, half)
    def _(i):
        second(i).wait_recv()
        finish((1 - odd) * half + i, r2[i])

    sib_copy(tp).wait_send()
    for c in range(CHUNKS):
        for j in range(1, chips):
            y_copy(j, c, tp).wait_send()
            pass_on(j, c, origin(j) * 2 + core).wait_send()

    @pl.loop(0, half)
    def _(i):
        first(i).wait_send()
        second(i).wait_send()

        @pl.when(pair < pairs - 1)
        def _():
            onward(i).wait_send()


def body(nctx, ntp, tokens, w_query, w_key, w_value, norm_gain):
    rows, depth = tokens.shape
    width = w_query.shape[1]
    heads = width // HEAD_DIM
    half, chips = heads // 2, ntp // 2
    tiles = width // TILE_N
    assert rows * ntp == BLOCK
    anywhere = pl.BlockSpec(memory_space=pl.ANY)
    vmem = pl.BlockSpec(memory_space=pltpu.VMEM)
    dma = pltpu.SemaphoreType.DMA
    small = pltpu.VMEM((half, HEAD_DIM, HEAD_DIM), BF16)
    hops = (max(chips - 1, 1), CHUNKS)
    return pl.pallas_call(
        functools.partial(kernel, nctx, ntp),
        out_shape=jax.ShapeDtypeStruct((BLOCK, width), BF16),
        in_specs=[anywhere] * 4 + [vmem],
        out_specs=vmem,
        scratch_shapes=[
            pltpu.VMEM((BLOCK, depth), BF16),
            pltpu.VMEM((3, depth, width), BF16),
            pltpu.VMEM((3, BLOCK, width), F32),
            pltpu.VMEM((3, BLOCK, width), BF16),
            pltpu.VMEM((heads, BLOCK, HEAD_DIM), F32),
            pltpu.VMEM((heads, HEAD_DIM, HEAD_DIM), F32),
            small, small, small, small, small, small, small,
            dma((3 * tiles,)), dma, dma(hops), dma(hops), dma, dma, dma(hops), dma(hops),
            dma((half,)), dma((half,)), dma((half,)), dma((half,)), dma((half,)), dma((half,)),
        ],
        compiler_params=pltpu.CompilerParams(
            collective_id=0, has_side_effects=True, vmem_limit_bytes=60 * 2**20
        ),
        cost_estimate=pl.CostEstimate(
            flops=2 * BLOCK * depth * 3 * width, bytes_accessed=6 * depth * width, transcendentals=0
        ),
    )(tokens, w_query, w_key, w_value, norm_gain.reshape(heads, HEAD_DIM))


def solution(mesh):
    placed = (P(("ctx", "tp"), None), P(None, "tp"), P(None, "tp"), P(None, "tp"), P("tp"))
    return jax.shard_map(
        functools.partial(body, mesh.shape["ctx"], mesh.shape["tp"]),
        mesh=mesh, in_specs=placed, out_specs=P("ctx", "tp"), check_vma=False,
    )
```

```python
import functools

import jax
import jax.numpy as jnp
from jax import lax
from jax.experimental import pallas as pl
from jax.experimental.pallas import tpu as pltpu
from jax.sharding import PartitionSpec as P

HEAD_DIM = 128
BLOCK = 512
EPSILON = 1e-06
MESH = pl.DeviceIdType.MESH
SPLIT = 2
TILE_N = 512
TWELFTHS = (0, 4, 8, 10, 11, 12)
CHUNKS = len(TWELFTHS) - 1
F32 = jnp.float32
BF16 = jnp.bfloat16


def kernel(
    nctx, ntp, tok, wq, wk, wv, gain, out,
    xbuf, wbuf, acc, kvq, mixed, st, s1, r1, pin, pout, pown, s2, r2,
    wsem, osem, ysend, yrecv, ssend, srecv, fsend, frecv,
    s1send, s1recv, csend, crecv, s2send, s2recv,
):
    ctx, tp = lax.axis_index("ctx"), lax.axis_index("tp")
    rows, depth = tok.shape
    width = wq.shape[1]
    tiles = width // TILE_N
    heads = width // HEAD_DIM
    half = heads // 2
    chips, pairs = ntp // 2, nctx // 2
    core, chip = tp % 2, tp // 2
    sib = tp + 1 - 2 * core
    odd, pair = ctx % 2, ctx // 2
    partner = ctx + 1 - 2 * odd
    cuts = [depth * part // 12 for part in TWELFTHS]
    duo = 2 * rows

    def at_rows(index, count):
        return pl.ds(pl.multiple_of(index * count, count), count)

    weights = (wk, wv, wq)

    def weight_copy(m, n):
        cols = pl.ds(pl.multiple_of(n * TILE_N, TILE_N), TILE_N)
        return pltpu.make_async_copy(
            weights[m].at[:, cols], wbuf.at[m, :, cols], wsem.at[m * tiles + n]
        )

    own = pltpu.make_async_copy(tok, xbuf.at[at_rows(tp, rows), :], osem)
    own.start()
    for m in range(3):
        for n in range(tiles):
            weight_copy(m, n).start()

    barrier = pltpu.get_barrier_semaphore()

    def greet(c, t):
        pl.semaphore_signal(barrier, inc=1, device_id={"ctx": c, "tp": t}, device_id_type=MESH)

    greet(ctx, sib)
    for j in range(1, chips):
        greet(ctx, ((chip + j) % chips) * 2 + core)
    greet(partner, tp)

    @pl.when(pair > 0)
    def _():
        greet(ctx - 2, tp)

    @pl.when(pair < pairs - 1)
    def _():
        greet(ctx + 2, tp)

    inner = jnp.minimum(pair, 1) + jnp.minimum(pairs - 1 - pair, 1)
    pl.semaphore_wait(barrier, chips + 1 + inner)

    def cols_of(c):
        return pl.ds(cuts[c], cuts[c + 1] - cuts[c])

    def y_copy(j, c, source):
        return pltpu.make_async_remote_copy(
            src_ref=tok.at[:, cols_of(c)],
            dst_ref=xbuf.at[at_rows(source, rows), cols_of(c)],
            send_sem=ysend.at[j - 1, c],
            recv_sem=yrecv.at[j - 1, c],
            device_id={"ctx": ctx, "tp": ((chip + j) % chips) * 2 + core},
            device_id_type=MESH,
        )

    def sib_copy(source):
        return pltpu.make_async_remote_copy(
            src_ref=tok,
            dst_ref=xbuf.at[at_rows(source, rows), :],
            send_sem=ssend,
            recv_sem=srecv,
            device_id={"ctx": ctx, "tp": sib},
            device_id_type=MESH,
        )

    def pass_on(j, c, source):
        place = xbuf.at[at_rows(source, rows), cols_of(c)]
        return pltpu.make_async_remote_copy(
            src_ref=place,
            dst_ref=place,
            send_sem=fsend.at[j - 1, c],
            recv_sem=frecv.at[j - 1, c],
            device_id={"ctx": ctx, "tp": sib},
            device_id_type=MESH,
        )

    for c in range(CHUNKS):
        for j in range(1, chips):
            y_copy(j, c, tp).start()
    sib_copy(tp).start()

    own.wait()
    sib_copy(sib).wait_recv()
    mine = at_rows(chip, duo)
    for m in range(3):

        @pl.loop(0, tiles)
        def _(n, m=m):
            weight_copy(m, n).wait()
            cols = pl.ds(pl.multiple_of(n * TILE_N, TILE_N), TILE_N)
            done = jnp.dot(xbuf[mine, :], wbuf[m, :, cols], preferred_element_type=F32)
            kvq[m, mine, cols] = done.astype(BF16)

    def head_cols(h):
        return pl.ds(pl.multiple_of(h * HEAD_DIM, HEAD_DIM), HEAD_DIM)

    def outer(h, where):
        return lax.dot_general(
            kvq[0, where, head_cols(h)], kvq[1, where, head_cols(h)],
            (((0,), (0,)), ((), ())), preferred_element_type=F32,
        )

    def whole_outer(h):
        total = st[h]
        for j in range(1, chips):
            total += outer(h, at_rows(origin(j), duo))
        return total

    @pl.loop(0, heads)
    def _(h):
        st[h] = outer(h, mine)

    def origin(j):
        return (chip - j + chips) % chips

    def wave(c, low, high):
        for j in range(1, chips):
            there = at_rows(origin(j), duo)

            @pl.loop(low, high)
            def _(m):
                term = jnp.dot(
                    xbuf[there, cols_of(c)], wbuf[m, cols_of(c), :], preferred_element_type=F32
                )
                if c > 0:
                    term += acc[m, there, :]
                if c < CHUNKS - 1:
                    acc[m, there, :] = term
                else:
                    kvq[m, there, :] = term.astype(BF16)

    for c in range(CHUNKS):
        for j in range(1, chips):
            source = origin(j) * 2 + core
            y_copy(j, c, source).wait_recv()
            pass_on(j, c, source).start()
        for j in range(1, chips):
            pass_on(j, c, origin(j) * 2 + 1 - core).wait_recv()
        if c < CHUNKS - 1:
            wave(c, 0, 3)
        else:
            wave(c, 0, 2)

    part = HEAD_DIM // SPLIT

    def piece(i):
        return i // SPLIT, pl.ds(pl.multiple_of((i % SPLIT) * part, part), part)

    def to_partner(buffer, landing, send, recv, i):
        return pltpu.make_async_remote_copy(
            src_ref=buffer.at[piece(i)],
            dst_ref=landing.at[piece(i)],
            send_sem=send.at[i],
            recv_sem=recv.at[i],
            device_id={"ctx": partner, "tp": tp},
            device_id_type=MESH,
        )

    def first(i):
        return to_partner(s1, r1, s1send, s1recv, i)

    def second(i):
        return to_partner(s2, r2, s2send, s2recv, i)

    def onward(i):
        return pltpu.make_async_remote_copy(
            src_ref=pout.at[piece(i)],
            dst_ref=pin.at[piece(i)],
            send_sem=csend.at[i],
            recv_sem=crecv.at[i],
            device_id={"ctx": jnp.minimum(ctx + 2, nctx - 2 + odd), "tp": tp},
            device_id_type=MESH,
        )

    @pl.loop(0, half)
    def _(i):
        s1[i] = whole_outer((1 - odd) * half + i).astype(BF16)
        for k in range(SPLIT):
            first(SPLIT * i + k).start()

    @pl.loop(0, half)
    def _(i):
        h = odd * half + i
        st[h] = whole_outer(h)

    wave(CHUNKS - 1, 2, 3)

    mid = BLOCK // 2

    def intra(h):
        cols = head_cols(h)
        causal = lax.broadcasted_iota(jnp.int32, (mid, mid), 0) >= lax.broadcasted_iota(
            jnp.int32, (mid, mid), 1
        )
        top, low = pl.ds(0, mid), pl.ds(mid, mid)

        def score(a, b):
            return lax.dot_general(
                kvq[2, a, cols], kvq[0, b, cols],
                (((1,), (1,)), ((), ())), preferred_element_type=F32,
            )

        s00 = jnp.where(causal, score(top, top), 0.0).astype(BF16)
        s10 = score(low, top).astype(BF16)
        s11 = jnp.where(causal, score(low, low), 0.0).astype(BF16)
        v0, v1 = kvq[1, top, cols], kvq[1, low, cols]
        mixed[h, top, :] = jnp.dot(s00, v0, preferred_element_type=F32)
        mixed[h, low, :] = jnp.dot(s10, v0, preferred_element_type=F32) + jnp.dot(
            s11, v1, preferred_element_type=F32
        )

    def finish(h, state):
        cols = head_cols(h)
        full = mixed[h] + jnp.dot(kvq[2, :, cols], state, preferred_element_type=F32)
        mean_square = jnp.mean(full * full, axis=-1, keepdims=True)
        out[:, cols] = (full * lax.rsqrt(mean_square + EPSILON) * gain[pl.ds(h, 1), :]).astype(BF16)

    @pl.when(pair == 0)
    def _():
        pin[...] = jnp.zeros_like(pin)

    ahead = jnp.minimum(3 * pair, heads)

    @pl.loop(0, ahead)
    def _(h):
        intra(h)

    @pl.loop(0, SPLIT * half)
    def _(i):
        first(i).wait_recv()

        @pl.when(pair > 0)
        def _():
            onward(i).wait_recv()

        spot = piece(i)
        before = pin[spot].astype(F32)
        here, beside = st[odd * half + spot[0], spot[1]], r1[spot].astype(F32)

        @pl.when(pair < pairs - 1)
        def _():
            pout[spot] = (before + here + beside).astype(BF16)
            onward(i).start()

        s2[spot] = (before + jnp.where(odd == 0, here, 0.0)).astype(BF16)
        second(i).start()
        pown[spot] = (before + jnp.where(odd == 1, beside, 0.0)).astype(BF16)

    @pl.loop(ahead, heads)
    def _(h):
        intra(h)

    @pl.loop(0, half)
    def _(i):
        finish(odd * half + i, pown[i])

    @pl.loop(0, half)
    def _(i):
        for k in range(SPLIT):
            second(SPLIT * i + k).wait_recv()
        finish((1 - odd) * half + i, r2[i])

    sib_copy(tp).wait_send()
    for c in range(CHUNKS):
        for j in range(1, chips):
            y_copy(j, c, tp).wait_send()
            pass_on(j, c, origin(j) * 2 + core).wait_send()

    @pl.loop(0, SPLIT * half)
    def _(i):
        first(i).wait_send()
        second(i).wait_send()

        @pl.when(pair < pairs - 1)
        def _():
            onward(i).wait_send()


def body(nctx, ntp, tokens, w_query, w_key, w_value, norm_gain):
    rows, depth = tokens.shape
    width = w_query.shape[1]
    heads = width // HEAD_DIM
    half, chips = heads // 2, ntp // 2
    tiles = width // TILE_N
    assert rows * ntp == BLOCK
    anywhere = pl.BlockSpec(memory_space=pl.ANY)
    vmem = pl.BlockSpec(memory_space=pltpu.VMEM)
    dma = pltpu.SemaphoreType.DMA
    small = pltpu.VMEM((half, HEAD_DIM, HEAD_DIM), BF16)
    hops = (max(chips - 1, 1), CHUNKS)
    return pl.pallas_call(
        functools.partial(kernel, nctx, ntp),
        out_shape=pltpu.VMEM((BLOCK, width), BF16),
        in_specs=[anywhere] * 4 + [vmem],
        out_specs=vmem,
        scratch_shapes=[
            pltpu.VMEM((BLOCK, depth), BF16),
            pltpu.VMEM((3, depth, width), BF16),
            pltpu.VMEM((3, BLOCK, width), F32),
            pltpu.VMEM((3, BLOCK, width), BF16),
            pltpu.VMEM((heads, BLOCK, HEAD_DIM), F32),
            pltpu.VMEM((heads, HEAD_DIM, HEAD_DIM), F32),
            small, small, small, small, small, small, small,
            dma((3 * tiles,)), dma, dma(hops), dma(hops), dma, dma, dma(hops), dma(hops),
            *[dma((SPLIT * half,))] * 6,
        ],
        compiler_params=pltpu.CompilerParams(
            collective_id=0, has_side_effects=True, vmem_limit_bytes=48 * 2**20
        ),
        cost_estimate=pl.CostEstimate(
            flops=2 * BLOCK * depth * 3 * width, bytes_accessed=6 * depth * width, transcendentals=0
        ),
    )(tokens, w_query, w_key, w_value, norm_gain.reshape(heads, HEAD_DIM))


def solution(mesh):
    placed = (P(("ctx", "tp"), None), P(None, "tp"), P(None, "tp"), P(None, "tp"), P("tp"))
    return jax.shard_map(
        functools.partial(body, mesh.shape["ctx"], mesh.shape["tp"]),
        mesh=mesh, in_specs=placed, out_specs=P("ctx", "tp"), check_vma=False,
    )
```
